32 devices in a mesh: ha: 8 (over y, x, core), wa: 4 (over z).
Axes of the slice: x: 2, y: 2, z: 4, core: 2. Of those that a mesh axis runs over, the one named last changes fastest.
Arguments:
- features: bfloat16 [7, 40, 80, 384], P(None, 'ha', 'wa'), may hold values from -6 to 6
- conv_weight: bfloat16 [10368, 384], P(('ha', 'wa')), may hold values from -0.0625 to 0.0625
- upconv_weight: bfloat16 [3456, 384], P(('ha', 'wa')), may hold values from -0.109375 to 0.109375
- norm_gain: bfloat16 [384], P(('ha', 'wa')), may hold values from 0.099609375 to 1.8984375
- cotangent: bfloat16 [5, 80, 160, 384], P(None, 'ha', 'wa'), may hold values from -6 to 6
Outputs:
- feature_grad: bfloat16 [7, 40, 80, 384], P(None, 'ha', 'wa')
- conv_grad: float32 [10368, 384], P(('ha', 'wa'))
- upconv_grad: float32 [3456, 384], P(('ha', 'wa'))
- gain_grad: float32 [384], P(('ha', 'wa'))
The draws below stay inside these ranges and needn't reach their ends.
All inputs are finite; a program needn't handle non-finite values.
Results may differ from the reference program's by a relative error of at most 0.005.
Values may be sent and summed in bfloat16 or wider, within the bound.
A program may use at most 192 MiB of HBM per device.

```python
import jax
import jax.numpy as jnp
from jax import lax

CHANNELS = 384
FRAMES = 5
HEIGHT = 40
WIDTH = 80


def with_spikes(entries, rng, source, target, shards_of, factor):
    def block_of(axis_at):
        return (jnp.arange(entries.shape[axis_at]) // (entries.shape[axis_at] // shards_of)).reshape((-1,) + (1,) * (entries.ndim - 1 - axis_at))

    one_side = jax.random.permutation(rng, shards_of)[block_of(target)]
    second = (block_of(target) + shards_of // 2) % shards_of
    return jnp.where((block_of(source) == one_side) | (block_of(source) == second), factor * entries, entries)


def levels(stream_key, dims, split, smallest, top_value):
    level, own = 1.0, jax.random.fold_in(stream_key, 6)
    for dim, shards_of in split:
        heights = jnp.exp(jax.random.uniform(jax.random.fold_in(own, dim), (shards_of,), jnp.float32, smallest / len(split), top_value / len(split)))
        level = level * jnp.repeat(heights, dims[dim] // shards_of).reshape([-1 if axis == dim else 1 for axis in range(len(dims))])
    return level


def scatter_about(stream_key, dims, scale, bound, split=(), kind=jnp.bfloat16):
    result = scale * jax.random.normal(stream_key, dims, jnp.float32)
    if split:
        result = result * levels(stream_key, dims, split, -0.22, 0.18)
    return jnp.clip(result, -bound, bound).astype(kind)


def heavy_noise(own_key, extent, width, limit, cuts, heavy, kind=jnp.bfloat16):
    result = width * jax.random.normal(own_key, extent, jnp.float32)
    if cuts:
        result = result * levels(own_key, extent, cuts, -0.22, 0.18)
    return jnp.clip(with_spikes(result, jax.random.fold_in(own_key, 3), *heavy), -limit, limit).astype(kind)


def setup_inputs(seed: int = 0) -> dict:
    key_of = jax.random.split(jax.random.key(seed), 6)
    features = heavy_noise(key_of[0], (FRAMES + 2, HEIGHT, WIDTH, CHANNELS), 1.0, 6.0, ((1, 8), (2, 4)), (1, 3, 8, 2.0))
    conv_weight = scatter_about(key_of[1], (27 * CHANNELS, CHANNELS), (27 * CHANNELS) ** -0.5, 0.0625, ((0, 32),))
    upconv_weight = scatter_about(key_of[2], (9 * CHANNELS, CHANNELS), (9 * CHANNELS) ** -0.5, 0.109375, ((0, 32),))
    norm_gain = jnp.clip(1.0 + 0.18 * jax.random.normal(key_of[3], (CHANNELS,), jnp.float32), 0.099609375, 1.8984375).astype(jnp.bfloat16)
    cotangent = scatter_about(key_of[4], (FRAMES, 2 * HEIGHT, 2 * WIDTH, CHANNELS), 1.0, 6.0, ((1, 8), (2, 4)))
    return dict(features=features, conv_weight=conv_weight, upconv_weight=upconv_weight, norm_gain=norm_gain, cotangent=cotangent)


EPSILON = 1e-06

def tap_blocks(weight, channels, flipped):
    blocks = weight.reshape(-1, channels, channels)
    if flipped:
        blocks = jnp.swapaxes(blocks, 1, 2)
    return blocks

def conv_taps(padded, blocks, out_frames, out_rows, out_cols, depth, flipped):
    channels = padded.shape[-1]
    outputs = blocks.shape[-1]
    total = jnp.zeros((out_frames * out_rows * out_cols, outputs), jnp.float32)
    for time_tap in range(depth):
        for row_tap in range(3):
            for col_tap in range(3):
                index_tap = (time_tap * 3 + row_tap) * 3 + col_tap
                if flipped:
                    time_from, row_from, col_from = (depth - 1 - time_tap, 2 - row_tap, 2 - col_tap)
                else:
                    time_from, row_from, col_from = (time_tap, row_tap, col_tap)
                window = padded[time_from:time_from + out_frames, row_from:row_from + out_rows, col_from:col_from + out_cols]
                total = total + jnp.dot(window.reshape(-1, channels), blocks[index_tap], preferred_element_type=jnp.float32)
    return total.reshape(out_frames, out_rows, out_cols, outputs)

def weight_grads(padded, cotan, out_frames, out_rows, out_cols, depth):
    channels = padded.shape[-1]
    flat_cot = cotan.reshape(-1, cotan.shape[-1])
    pieces = []
    for time_tap in range(depth):
        for row_tap in range(3):
            for col_tap in range(3):
                window = padded[time_tap:time_tap + out_frames, row_tap:row_tap + out_rows, col_tap:col_tap + out_cols]
                pieces.append(lax.dot_general(window.reshape(-1, channels), flat_cot, (((0,), (0,)), ((), ())), preferred_element_type=jnp.float32))
    return jnp.concatenate(pieces, axis=0)

def norm_parts(hidden, gain):
    inverse = lax.rsqrt(lax.optimization_barrier(jnp.mean(hidden * hidden, axis=-1, keepdims=True)) + EPSILON)
    return (inverse, hidden * inverse * gain.astype(jnp.float32))

def norm_backward(hidden, inverse, normed, gain, grad_act):
    sigmoid_v = jax.nn.sigmoid(normed)
    grad_norm = grad_act * sigmoid_v * (1.0 + normed * (1.0 - sigmoid_v))
    gain_terms = lax.optimization_barrier(jnp.sum(grad_norm * hidden * inverse, axis=(0, 1, 2)))
    grad_q = grad_norm * gain.astype(jnp.float32)
    centre = lax.optimization_barrier(jnp.mean(grad_q * hidden, axis=-1, keepdims=True))
    grad_hidden = (inverse * (grad_q - hidden * inverse * inverse * centre)).astype(jnp.bfloat16)
    return (grad_hidden, gain_terms)

def upsample(active):
    frames, height, breadth, channels = active.shape
    spread = jnp.broadcast_to(active[:, :, None, :, None, :], (frames, height, 2, breadth, 2, channels))
    return spread.reshape(frames, 2 * height, 2 * breadth, channels)

def reference(features, conv_weight, upconv_weight, norm_gain, cotangent):
    channels = features.shape[-1]
    frames = cotangent.shape[0]
    height = features.shape[1]
    breadth = features.shape[2]
    factor = 1.0 / (frames * height * breadth) ** 0.5
    padded = jnp.pad(features, ((0, 0), (1, 1), (1, 1), (0, 0)))
    hidden = conv_taps(padded, tap_blocks(conv_weight, channels, False), frames, height, breadth, 3, False)
    inverse, normed = norm_parts(hidden, norm_gain)
    active = jax.nn.silu(normed).astype(jnp.bfloat16)
    upsampled = jnp.pad(upsample(active), ((0, 0), (1, 1), (1, 1), (0, 0)))
    cot_pad = jnp.pad(cotangent, ((0, 0), (1, 1), (1, 1), (0, 0)))
    grad_up = conv_taps(cot_pad, tap_blocks(upconv_weight, channels, True), frames, 2 * height, 2 * breadth, 1, True)
    grad_act = grad_up.reshape(frames, height, 2, breadth, 2, channels).sum(axis=(2, 4))
    grad_hidden, gain_terms = norm_backward(hidden, inverse, normed, norm_gain, grad_act)
    grad_pad = jnp.pad(grad_hidden, ((2, 2), (1, 1), (1, 1), (0, 0)))
    feature_grad = conv_taps(grad_pad, tap_blocks(conv_weight, channels, True), frames + 2, height, breadth, 3, True).astype(jnp.bfloat16)
    conv_grad = weight_grads(padded, grad_hidden, frames, height, breadth, 3) * factor
    upconv_grad = weight_grads(upsampled, cotangent, frames, 2 * height, 2 * breadth, 1) * (0.5 * factor)
    gain_grad = gain_terms * factor
    return (feature_grad, conv_grad, upconv_grad, gain_grad)
```

```python
import math

import jax
import jax.numpy as jnp
from jax import lax
from jax.sharding import PartitionSpec as P

EPSILON = 1e-06


def with_halo(block, sides):
    for axis, dim in sides:
        count = lax.axis_size(axis)
        forward = [(i, i + 1) for i in range(count - 1)]
        backward = [(target, source) for source, target in forward]
        low = lax.ppermute(
            lax.slice_in_dim(block, block.shape[dim] - 1, None, axis=dim), axis, forward
        )
        high = lax.ppermute(lax.slice_in_dim(block, 0, 1, axis=dim), axis, backward)
        block = jnp.concatenate([low, block, high], axis=dim)
    return block


def flat_cells(window, plane):
    frames, height, breadth, channels = window.shape
    cells = window.reshape(frames, height * breadth, channels)
    return jnp.pad(cells, ((0, 0), (0, plane - height * breadth), (0, 0)))


def spatial_taps(wide, height, breadth, plane, flipped):
    pieces = []
    for row_tap in range(3):
        for col_tap in range(3):
            b, c = (2 - row_tap, 2 - col_tap) if flipped else (row_tap, col_tap)
            pieces.append(flat_cells(wide[:, b : b + height, c : c + breadth], plane))
    return jnp.concatenate(pieces, axis=-1)


def halve(block, axis, bits, left):
    count = lax.axis_size(axis)
    me = lax.axis_index(axis)
    left = list(left)
    for bit in bits:
        place = left.index(bit)
        mine = (me >> bit) & 1
        send = lax.dynamic_index_in_dim(block, 1 - mine, place, keepdims=False)
        keep = lax.dynamic_index_in_dim(block, mine, place, keepdims=False)
        got = lax.ppermute(
            send.astype(jnp.bfloat16), axis, [(i, i ^ (1 << bit)) for i in range(count)]
        )
        block = keep.astype(jnp.float32) + got.astype(jnp.float32)
        left.remove(bit)
    return block


def bits_of(count):
    return list(range(count.bit_length() - 1))


def body(features, conv_weight, upconv_weight, norm_gain, cotangent):
    f32, bf16 = jnp.float32, jnp.bfloat16
    frames = cotangent.shape[0]
    frames_in, height, breadth, channels = features.shape
    n_ha, n_wa = lax.axis_size("ha"), lax.axis_size("wa")
    cells = height * breadth
    plane = -(-cells // 16) * 16
    factor = 1.0 / math.sqrt(frames * cells * n_ha * n_wa)
    ha_bits, wa_bits = bits_of(n_ha), bits_of(n_wa)
    own_gain = norm_gain.shape[0]
    up_rows = upconv_weight.shape[0]
    sides = (("ha", 1), ("wa", 2))

    gain_row = jnp.pad(norm_gain[None, :], ((0, 3), (0, channels - own_gain)))
    packed = lax.all_gather(
        jnp.concatenate([upconv_weight, gain_row], axis=0), ("ha", "wa"), axis=0, tiled=False
    )
    second = packed[:, :up_rows].reshape(3, 3, channels, channels).astype(f32)
    gain = packed[:, up_rows, :own_gain].reshape(channels).astype(f32)
    first = lax.all_gather(conv_weight, ("ha", "wa"), axis=0, tiled=True)

    cot_wide = with_halo(cotangent, sides)
    pairs = cot_wide.reshape(frames, height + 1, 2, breadth + 1, 2 * channels)
    pieces = []
    for d in range(4):
        for off in range(2):
            window = pairs[:, d // 2 : d // 2 + height, d % 2, off : off + breadth]
            pieces.append(flat_cells(window, plane))
    cot_taps = jnp.concatenate(pieces, axis=-1).reshape(frames * plane, 16 * channels)
    turned = jnp.swapaxes(second, 2, 3)
    rows = [turned[2], turned[1] + turned[2], turned[0] + turned[1], turned[0]]
    mixed = [
        jnp.stack([row[2], row[1] + row[2], row[0] + row[1], row[0]]) for row in rows
    ]
    mixed = jnp.stack(mixed).astype(bf16).reshape(16 * channels, channels)
    grad_act = jnp.dot(cot_taps, mixed, preferred_element_type=f32)

    wide = with_halo(features, sides)
    taps = spatial_taps(wide, height, breadth, plane, False).reshape(
        frames_in * plane, 9 * channels
    )
    size = 9 * channels
    length = frames * plane
    hidden = jnp.zeros((length, channels), f32)
    for a in range(3):
        hidden = hidden + jnp.dot(
            taps[a * plane : a * plane + length],
            first[a * size : (a + 1) * size],
            preferred_element_type=f32,
        )

    inverse = lax.rsqrt(jnp.mean(hidden * hidden, axis=-1, keepdims=True) + EPSILON)
    normed = hidden * inverse * gain
    sigmoid_v = jax.nn.sigmoid(normed)
    active = (normed * sigmoid_v).astype(bf16)
    grad_norm = grad_act * sigmoid_v * (1.0 + normed * (1.0 - sigmoid_v))
    gain_terms = jnp.sum(grad_norm * hidden * inverse, axis=0)
    grad_q = grad_norm * gain
    centre = jnp.mean(grad_q * hidden, axis=-1, keepdims=True)
    grad_hidden = (inverse * (grad_q - hidden * inverse * inverse * centre)).astype(bf16)

    over_rows = (((0,), (0,)), ((), ()))
    local_first = jnp.concatenate(
        [
            (
                lax.dot_general(
                    taps[a * plane : a * plane + length],
                    grad_hidden,
                    over_rows,
                    preferred_element_type=f32,
                )
                * factor
            ).astype(bf16)
            for a in range(3)
        ],
        axis=0,
    )
    cross = lax.dot_general(active, cot_taps, over_rows, preferred_element_type=f32)
    cross = [
        [cross[:, (4 * d + e) * channels : (4 * d + e + 1) * channels] for e in range(4)]
        for d in range(4)
    ]
    local_second = jnp.concatenate(
        [
            (
                (
                    cross[2 - b][2 - c]
                    + cross[2 - b][3 - c]
                    + cross[3 - b][2 - c]
                    + cross[3 - b][3 - c]
                )
                * (0.5 * factor)
            ).astype(bf16)
            for b in range(3)
            for c in range(3)
        ],
        axis=0,
    )
    up_part = local_second.shape[0] // n_ha
    gain_rows = -(-n_wa // 16) * 16
    gain_part = jnp.pad(
        (gain_terms * factor).astype(bf16).reshape(n_ha, n_wa, own_gain),
        ((0, 0), (0, gain_rows - n_wa), (0, channels - own_gain)),
    )
    small = jnp.concatenate([local_second.reshape(n_ha, up_part, channels), gain_part], axis=1)
    small = small.reshape((2,) * len(ha_bits) + small.shape[1:])
    small = halve(small, "ha", ha_bits, ha_bits[::-1])
    ups = small[:up_part].reshape(n_wa, up_rows, channels)
    small = jnp.concatenate([ups, small[up_part : up_part + n_wa][:, None]], axis=1)
    small = small.reshape((2,) * len(wa_bits) + small.shape[1:])
    small = halve(small, "wa", wa_bits, wa_bits[::-1])
    upconv_grad = small[:up_rows]
    gain_grad = small[up_rows, :own_gain]

    part = local_first.shape[0] // n_ha
    big = local_first.reshape((2,) * len(ha_bits) + (part, channels))
    big = halve(big, "ha", [0], ha_bits[::-1])
    left = ha_bits[:0:-1]
    ends = []
    for side, order in ((0, ha_bits[1:]), (1, left)):
        half = big[..., side * part // 2 : (side + 1) * part // 2, :]
        ends.append(halve(half, "ha", order, left))
    big = jnp.stack(ends).reshape((2,) * len(wa_bits) + (part // n_wa, channels))
    conv_grad = halve(big, "wa", wa_bits, wa_bits[::-1])

    grad_wide = with_halo(
        grad_hidden.reshape(frames, plane, channels)[:, :cells].reshape(
            frames, height, breadth, channels
        ),
        sides,
    )
    grad_taps = spatial_taps(grad_wide, height, breadth, plane, True)
    grad_taps = jnp.pad(grad_taps, ((2, 2), (0, 0), (0, 0))).reshape((frames + 4) * plane, size)
    turned = jnp.swapaxes(first.reshape(3, 9, channels, channels), 2, 3).reshape(3, size, channels)
    long = (frames + 2) * plane
    feature = jnp.zeros((long, channels), f32)
    for a in range(3):
        start = (2 - a) * plane
        feature = feature + jnp.dot(
            grad_taps[start : start + long], turned[a], preferred_element_type=f32
        )
    feature_grad = (
        feature.astype(bf16)
        .reshape(frames + 2, plane, channels)[:, :cells]
        .reshape(frames + 2, height, breadth, channels)
    )
    return (feature_grad, conv_grad, upconv_grad, gain_grad)


def solution(mesh):
    return jax.shard_map(
        body,
        mesh=mesh,
        in_specs=(
            P(None, "ha", "wa", None),
            P(("ha", "wa"), None),
            P(("ha", "wa"), None),
            P(("ha", "wa")),
            P(None, "ha", "wa", None),
        ),
        out_specs=(
            P(None, "ha", "wa", None),
            P(("ha", "wa"), None),
            P(("ha", "wa"), None),
            P(("ha", "wa")),
        ),
        check_vma=False,
    )
```

```python
import math

import jax
import jax.numpy as jnp
from jax import lax
from jax.sharding import PartitionSpec as P

EPSILON = 1e-06


def with_halo(block, sides):
    for axis, dim in sides:
        count = lax.axis_size(axis)
        forward = [(i, i + 1) for i in range(count - 1)]
        backward = [(target, source) for source, target in forward]
        low = lax.ppermute(
            lax.slice_in_dim(block, block.shape[dim] - 1, None, axis=dim), axis, forward
        )
        high = lax.ppermute(lax.slice_in_dim(block, 0, 1, axis=dim), axis, backward)
        block = jnp.concatenate([low, block, high], axis=dim)
    return block


def flat_cells(window, plane):
    frames, height, breadth, channels = window.shape
    cells = window.reshape(frames, height * breadth, channels)
    return jnp.pad(cells, ((0, 0), (0, plane - height * breadth), (0, 0)))


def spatial_taps(wide, height, breadth, plane, flipped):
    pieces = []
    for row_tap in range(3):
        for col_tap in range(3):
            b, c = (2 - row_tap, 2 - col_tap) if flipped else (row_tap, col_tap)
            pieces.append(flat_cells(wide[:, b : b + height, c : c + breadth], plane))
    return jnp.concatenate(pieces, axis=-1)


def halve(block, axis, bits, left):
    count = lax.axis_size(axis)
    me = lax.axis_index(axis)
    left = list(left)
    for bit in bits:
        place = left.index(bit)
        mine = (me >> bit) & 1
        send = lax.dynamic_index_in_dim(block, 1 - mine, place, keepdims=False)
        keep = lax.dynamic_index_in_dim(block, mine, place, keepdims=False)
        got = lax.ppermute(
            send.astype(jnp.bfloat16), axis, [(i, i ^ (1 << bit)) for i in range(count)]
        )
        block = keep.astype(jnp.float32) + got.astype(jnp.float32)
        left.remove(bit)
    return block


def bits_of(count):
    return list(range(count.bit_length() - 1))


def body(features, conv_weight, upconv_weight, norm_gain, cotangent):
    f32, bf16 = jnp.float32, jnp.bfloat16
    frames = cotangent.shape[0]
    frames_in, height, breadth, channels = features.shape
    n_ha, n_wa = lax.axis_size("ha"), lax.axis_size("wa")
    cells = height * breadth
    plane = -(-cells // 16) * 16
    factor = 1.0 / math.sqrt(frames * cells * n_ha * n_wa)
    ha_bits, wa_bits = bits_of(n_ha), bits_of(n_wa)
    own_gain = norm_gain.shape[0]
    up_rows = upconv_weight.shape[0]
    sides = (("ha", 1), ("wa", 2))

    gain_row = jnp.pad(norm_gain[None, :], ((0, 3), (0, channels - own_gain)))
    packed = lax.all_gather(
        jnp.concatenate([upconv_weight, gain_row], axis=0), ("ha", "wa"), axis=0, tiled=False
    )
    second = packed[:, :up_rows].reshape(3, 3, channels, channels).astype(f32)
    gain = packed[:, up_rows, :own_gain].reshape(channels).astype(f32)
    first = lax.all_gather(conv_weight, ("ha", "wa"), axis=0, tiled=True)

    cot_wide = with_halo(cotangent, sides)
    pairs = cot_wide.reshape(frames, height + 1, 2, breadth + 1, 2 * channels)
    pieces = []
    for d in range(4):
        for off in range(2):
            window = pairs[:, d // 2 : d // 2 + height, d % 2, off : off + breadth]
            pieces.append(flat_cells(window, plane))
    cot_taps = jnp.concatenate(pieces, axis=-1).reshape(frames * plane, 16 * channels)
    turned = jnp.swapaxes(second, 2, 3)
    rows = [turned[2], turned[1] + turned[2], turned[0] + turned[1], turned[0]]
    mixed = [
        jnp.stack([row[2], row[1] + row[2], row[0] + row[1], row[0]]) for row in rows
    ]
    mixed = jnp.stack(mixed).astype(bf16).reshape(16 * channels, channels)
    grad_act = jnp.dot(cot_taps, mixed, preferred_element_type=f32)

    wide = with_halo(features, sides)
    taps = spatial_taps(wide, height, breadth, plane, False).reshape(
        frames_in * plane, 9 * channels
    )
    size = 9 * channels
    length = frames * plane
    hidden = jnp.zeros((length, channels), f32)
    for a in range(3):
        hidden = hidden + jnp.dot(
            taps[a * plane : a * plane + length],
            first[a * size : (a + 1) * size],
            preferred_element_type=f32,
        )

    inverse = lax.rsqrt(jnp.mean(hidden * hidden, axis=-1, keepdims=True) + EPSILON)
    normed = hidden * inverse * gain
    sigmoid_v = jax.nn.sigmoid(normed)
    active = (normed * sigmoid_v).astype(bf16)
    grad_norm = grad_act * sigmoid_v * (1.0 + normed * (1.0 - sigmoid_v))
    gain_terms = jnp.sum(grad_norm * hidden * inverse, axis=0)
    grad_q = grad_norm * gain
    centre = jnp.mean(grad_q * hidden, axis=-1, keepdims=True)
    grad_hidden = (inverse * (grad_q - hidden * inverse * inverse * centre)).astype(bf16)

    over_rows = (((0,), (0,)), ((), ()))
    local_first = jnp.concatenate(
        [
            (
                lax.dot_general(
                    taps[a * plane : a * plane + length],
                    grad_hidden,
                    over_rows,
                    preferred_element_type=f32,
                )
                * factor
            ).astype(bf16)
            for a in range(3)
        ],
        axis=0,
    )
    cross = lax.dot_general(active, cot_taps, over_rows, preferred_element_type=f32)
    cross = [
        [cross[:, (4 * d + e) * channels : (4 * d + e + 1) * channels] for e in range(4)]
        for d in range(4)
    ]
    local_second = jnp.concatenate(
        [
            (
                (
                    cross[2 - b][2 - c]
                    + cross[2 - b][3 - c]
                    + cross[3 - b][2 - c]
                    + cross[3 - b][3 - c]
                )
                * (0.5 * factor)
            ).astype(bf16)
            for b in range(3)
            for c in range(3)
        ],
        axis=0,
    )
    up_part = local_second.shape[0] // n_ha
    gain_rows = -(-n_wa // 16) * 16
    gain_part = jnp.pad(
        (gain_terms * factor).astype(bf16).reshape(n_ha, n_wa, own_gain),
        ((0, 0), (0, gain_rows - n_wa), (0, channels - own_gain)),
    )
    small = jnp.concatenate([local_second.reshape(n_ha, up_part, channels), gain_part], axis=1)
    small = small.reshape((2,) * len(ha_bits) + small.shape[1:])
    small = halve(small, "ha", [0], ha_bits[::-1])

    part = local_first.shape[0] // n_ha
    big = local_first.reshape((2,) * len(ha_bits) + (part, channels))
    big = halve(big, "ha", [0], ha_bits[::-1])
    left = ha_bits[:0:-1]
    first, big, small = lax.optimization_barrier((first, big, small))
    small = halve(small, "ha", ha_bits[1:], left)
    ups = small[:up_part].reshape(n_wa, up_rows, channels)
    small = jnp.concatenate([ups, small[up_part : up_part + n_wa][:, None]], axis=1)
    small = small.reshape((2,) * len(wa_bits) + small.shape[1:])
    small = halve(small, "wa", wa_bits, wa_bits[::-1])
    upconv_grad = small[:up_rows]
    gain_grad = small[up_rows, :own_gain]

    ends = []
    for side, order in ((0, ha_bits[1:]), (1, left)):
        half = big[..., side * part // 2 : (side + 1) * part // 2, :]
        ends.append(halve(half, "ha", order, left))
    big = jnp.stack(ends).reshape((2,) * len(wa_bits) + (part // n_wa, channels))
    conv_grad = halve(big, "wa", wa_bits, wa_bits[::-1])

    grad_wide = with_halo(
        grad_hidden.reshape(frames, plane, channels)[:, :cells].reshape(
            frames, height, breadth, channels
        ),
        sides,
    )
    grad_taps = spatial_taps(grad_wide, height, breadth, plane, True)
    grad_taps = jnp.pad(grad_taps, ((2, 2), (0, 0), (0, 0))).reshape((frames + 4) * plane, size)
    turned = jnp.swapaxes(first.reshape(3, 9, channels, channels), 2, 3).reshape(3, size, channels)
    long = (frames + 2) * plane
    feature = jnp.zeros((long, channels), f32)
    for a in range(3):
        start = (2 - a) * plane
        feature = feature + jnp.dot(
            grad_taps[start : start + long], turned[a], preferred_element_type=f32
        )
    feature_grad = (
        feature.astype(bf16)
        .reshape(frames + 2, plane, channels)[:, :cells]
        .reshape(frames + 2, height, breadth, channels)
    )
    return (feature_grad, conv_grad, upconv_grad, gain_grad)


def solution(mesh):
    return jax.shard_map(
        body,
        mesh=mesh,
        in_specs=(
            P(None, "ha", "wa", None),
            P(("ha", "wa"), None),
            P(("ha", "wa"), None),
            P(("ha", "wa")),
            P(None, "ha", "wa", None),
        ),
        out_specs=(
            P(None, "ha", "wa", None),
            P(("ha", "wa"), None),
            P(("ha", "wa"), None),
            P(("ha", "wa")),
        ),
        check_vma=False,
    )
```

```python
import math

import jax
import jax.numpy as jnp
from jax import lax
from jax.sharding import PartitionSpec as P

EPSILON = 1e-06


def with_halo(block, sides):
    for axis, dim in sides:
        count = lax.axis_size(axis)
        forward = [(i, i + 1) for i in range(count - 1)]
        backward = [(target, source) for source, target in forward]
        low = lax.ppermute(
            lax.slice_in_dim(block, block.shape[dim] - 1, None, axis=dim), axis, forward
        )
        high = lax.ppermute(lax.slice_in_dim(block, 0, 1, axis=dim), axis, backward)
        block = jnp.concatenate([low, block, high], axis=dim)
    return block


def flat_cells(window, plane):
    frames, height, breadth, channels = window.shape
    cells = window.reshape(frames, height * breadth, channels)
    return jnp.pad(cells, ((0, 0), (0, plane - height * breadth), (0, 0)))


def spatial_taps(wide, height, breadth, plane, flipped):
    pieces = []
    for row_tap in range(3):
        for col_tap in range(3):
            b, c = (2 - row_tap, 2 - col_tap) if flipped else (row_tap, col_tap)
            pieces.append(flat_cells(wide[:, b : b + height, c : c + breadth], plane))
    return jnp.concatenate(pieces, axis=-1)


def halve(block, axis, bits, left):
    count = lax.axis_size(axis)
    me = lax.axis_index(axis)
    left = list(left)
    for bit in bits:
        place = left.index(bit)
        mine = (me >> bit) & 1
        send = lax.dynamic_index_in_dim(block, 1 - mine, place, keepdims=False)
        keep = lax.dynamic_index_in_dim(block, mine, place, keepdims=False)
        got = lax.ppermute(
            send.astype(jnp.bfloat16), axis, [(i, i ^ (1 << bit)) for i in range(count)]
        )
        block = keep.astype(jnp.float32) + got.astype(jnp.float32)
        left.remove(bit)
    return block


def bits_of(count):
    return list(range(count.bit_length() - 1))


def body(features, conv_weight, upconv_weight, norm_gain, cotangent):
    f32, bf16 = jnp.float32, jnp.bfloat16
    frames = cotangent.shape[0]
    frames_in, height, breadth, channels = features.shape
    n_ha, n_wa = lax.axis_size("ha"), lax.axis_size("wa")
    cells = height * breadth
    plane = -(-cells // 16) * 16
    factor = 1.0 / math.sqrt(frames * cells * n_ha * n_wa)
    ha_bits, wa_bits = bits_of(n_ha), bits_of(n_wa)
    own_gain = norm_gain.shape[0]
    up_rows = upconv_weight.shape[0]
    sides = (("ha", 1), ("wa", 2))

    gain_row = jnp.pad(norm_gain[None, :], ((0, 3), (0, channels - own_gain)))
    packed = lax.all_gather(
        jnp.concatenate([upconv_weight, gain_row], axis=0), ("ha", "wa"), axis=0, tiled=False
    )
    second = packed[:, :up_rows].reshape(3, 3, channels, channels).astype(f32)
    gain = packed[:, up_rows, :own_gain].reshape(channels).astype(f32)
    first = lax.all_gather(conv_weight, ("ha", "wa"), axis=0, tiled=True)

    cot_wide = with_halo(cotangent, sides)
    pairs = cot_wide.reshape(frames, height + 1, 2, breadth + 1, 2 * channels)
    pieces = []
    for d in range(4):
        for off in range(2):
            window = pairs[:, d // 2 : d // 2 + height, d % 2, off : off + breadth]
            pieces.append(flat_cells(window, plane))
    cot_taps = jnp.concatenate(pieces, axis=-1).reshape(frames * plane, 16 * channels)
    turned = jnp.swapaxes(second, 2, 3)
    rows = [turned[2], turned[1] + turned[2], turned[0] + turned[1], turned[0]]
    mixed = [
        jnp.stack([row[2], row[1] + row[2], row[0] + row[1], row[0]]) for row in rows
    ]
    mixed = jnp.stack(mixed).astype(bf16).reshape(16 * channels, channels)
    grad_act = jnp.dot(cot_taps, mixed, preferred_element_type=f32)

    wide = with_halo(features, sides)
    taps = spatial_taps(wide, height, breadth, plane, False).reshape(
        frames_in * plane, 9 * channels
    )
    size = 9 * channels
    length = frames * plane
    hidden = jnp.zeros((length, channels), f32)
    for a in range(3):
        hidden = hidden + jnp.dot(
            taps[a * plane : a * plane + length],
            first[a * size : (a + 1) * size],
            preferred_element_type=f32,
        )

    inverse = lax.rsqrt(jnp.mean(hidden * hidden, axis=-1, keepdims=True) + EPSILON)
    normed = hidden * inverse * gain
    sigmoid_v = jax.nn.sigmoid(normed)
    active = (normed * sigmoid_v).astype(bf16)
    grad_norm = grad_act * sigmoid_v * (1.0 + normed * (1.0 - sigmoid_v))
    gain_terms = jnp.sum(grad_norm * hidden * inverse, axis=0)
    grad_q = grad_norm * gain
    centre = jnp.mean(grad_q * hidden, axis=-1, keepdims=True)
    grad_hidden = (inverse * (grad_q - hidden * inverse * inverse * centre)).astype(bf16)

    over_rows = (((0,), (0,)), ((), ()))
    local_first = jnp.concatenate(
        [
            (
                lax.dot_general(
                    taps[a * plane : a * plane + length],
                    grad_hidden,
                    over_rows,
                    preferred_element_type=f32,
                )
                * factor
            ).astype(bf16)
            for a in range(3)
        ],
        axis=0,
    )
    cross = lax.dot_general(active, cot_taps, over_rows, preferred_element_type=f32)
    cross = [
        [cross[:, (4 * d + e) * channels : (4 * d + e + 1) * channels] for e in range(4)]
        for d in range(4)
    ]
    local_second = jnp.concatenate(
        [
            (
                (
                    cross[2 - b][2 - c]
                    + cross[2 - b][3 - c]
                    + cross[3 - b][2 - c]
                    + cross[3 - b][3 - c]
                )
                * (0.5 * factor)
            ).astype(bf16)
            for b in range(3)
            for c in range(3)
        ],
        axis=0,
    )
    up_part = local_second.shape[0] // n_ha
    gain_rows = -(-n_wa // 16) * 16
    gain_part = jnp.pad(
        (gain_terms * factor).astype(bf16).reshape(n_ha, n_wa, own_gain),
        ((0, 0), (0, gain_rows - n_wa), (0, channels - own_gain)),
    )
    small = jnp.concatenate([local_second.reshape(n_ha, up_part, channels), gain_part], axis=1)
    small = small.reshape((2,) * len(ha_bits) + small.shape[1:])
    small = halve(small, "ha", [0], ha_bits[::-1])

    part = local_first.shape[0] // n_ha
    big = local_first.reshape((2,) * len(ha_bits) + (part, channels))
    big = halve(big, "ha", [0], ha_bits[::-1])
    grad_wide = with_halo(
        grad_hidden.reshape(frames, plane, channels)[:, :cells].reshape(
            frames, height, breadth, channels
        ),
        sides,
    )
    left = ha_bits[:0:-1]
    grad_wide, big, small = lax.optimization_barrier((grad_wide, big, small))
    small = halve(small, "ha", ha_bits[1:], left)
    ups = small[:up_part].reshape(n_wa, up_rows, channels)
    small = jnp.concatenate([ups, small[up_part : up_part + n_wa][:, None]], axis=1)
    small = small.reshape((2,) * len(wa_bits) + small.shape[1:])
    small = halve(small, "wa", wa_bits, wa_bits[::-1])
    upconv_grad = small[:up_rows]
    gain_grad = small[up_rows, :own_gain]

    ends = []
    for side, order in ((0, ha_bits[1:]), (1, left)):
        half = big[..., side * part // 2 : (side + 1) * part // 2, :]
        ends.append(halve(half, "ha", order, left))
    big = jnp.stack(ends).reshape((2,) * len(wa_bits) + (part // n_wa, channels))
    conv_grad = halve(big, "wa", wa_bits, wa_bits[::-1])

    blocks = first.reshape(27, channels, channels)
    long = (frames + 2) * plane
    feature = jnp.zeros((long, channels), f32)
    for row_tap in range(3):
        for col_tap in range(3):
            b, c = 2 - row_tap, 2 - col_tap
            piece = flat_cells(grad_wide[:, b : b + height, c : c + breadth], plane)
            piece = jnp.pad(piece, ((2, 2), (0, 0), (0, 0))).reshape(-1, channels)
            for a in range(3):
                start = (2 - a) * plane
                feature = feature + lax.dot_general(
                    piece[start : start + long],
                    blocks[(a * 3 + row_tap) * 3 + col_tap],
                    (((1,), (1,)), ((), ())),
                    preferred_element_type=f32,
                )
    feature_grad = (
        feature.astype(bf16)
        .reshape(frames + 2, plane, channels)[:, :cells]
        .reshape(frames + 2, height, breadth, channels)
    )
    return (feature_grad, conv_grad, upconv_grad, gain_grad)


def solution(mesh):
    return jax.shard_map(
        body,
        mesh=mesh,
        in_specs=(
            P(None, "ha", "wa", None),
            P(("ha", "wa"), None),
            P(("ha", "wa"), None),
            P(("ha", "wa")),
            P(None, "ha", "wa", None),
        ),
        out_specs=(
            P(None, "ha", "wa", None),
            P(("ha", "wa"), None),
            P(("ha", "wa"), None),
            P(("ha", "wa")),
        ),
        check_vma=False,
    )
```
